512 devices in a mesh: row: 16 (over z), col: 32 (over y, x, core).
Axes of the slice: x: 4, y: 4, z: 16, core: 2. Of those that a mesh axis runs over, the one named last changes fastest.
Arguments:
- inputs: bfloat16 [768, 12288], P('col', 'row'), may hold values from -40 to 40
- ln_gain: float32 [12288], P('row'), may hold values from 0.25 to 1.75
- ln_bias: float32 [12288], P('row'), may hold values from -4 to 4
- w_up: bfloat16 [12288, 49152], P('row', 'col'), may hold values from -0.0546875 to 0.0546875
- up_bias: float32 [49152], P('col'), may hold values from -4 to 4
- w_down: bfloat16 [49152, 12288], P('col', 'row'), may hold values from -0.02734375 to 0.02734375
- down_bias: float32 [12288], P('row'), may hold values from -4 to 4
Outputs:
- block_out: bfloat16 [768, 12288], P('col', 'row')
The draws below stay inside these ranges and needn't reach their ends.
All inputs are finite; a program needn't handle non-finite values.
Results may differ from the reference program's by a relative error of at most 0.0085.
Values may be sent and summed in bfloat16 or wider, within the bound.
A program may use at most 64 MiB of HBM per device.

```python
import math
import jax
import jax.numpy as jnp
from jax import lax

D = 12288
FFW = 49152
TOKENS = 768
N_ROW = 16
N_COL = 32


def draw_inputs(key, part):
    key_base = jax.random.fold_in(key, 11)
    key_jitter = jax.random.fold_in(key, 12)
    key_rows = jax.random.fold_in(key, 13)
    key_offset = jax.random.fold_in(key, 14)
    key_sign = jax.random.fold_in(key, 15)
    key_start = jax.random.fold_in(key, 16)
    key_band_sign = jax.random.fold_in(key, 17)
    key_band_size = jax.random.fold_in(key, 18)
    position = jnp.arange(D, dtype=jnp.float32) / (D - 1)
    jitter = jax.random.uniform(key_jitter, (D,), jnp.float32, 0.0, math.log(3.3))
    col_scale = jnp.exp(math.log(3.0) * (position - 0.5) + jitter - 0.5 * math.log(3.3))
    row_scale = jnp.exp(jax.random.uniform(key_rows, (TOKENS, 1), jnp.float32, math.log(0.3), math.log(3.0)))
    sign = jnp.where(jax.random.uniform(key_sign, (TOKENS, 1), jnp.float32) < 0.5, -1.0, 1.0)
    band_width = max(D // 64, 1)
    band_count = D // band_width
    band_start = jax.random.randint(key_start, (), 0, band_count, dtype=jnp.int32) * band_width
    feature = jnp.arange(D, dtype=jnp.int32)
    in_band = jnp.logical_and(feature >= band_start, feature < band_start + band_width)
    band_sign = jnp.where(jax.random.uniform(key_band_sign, (TOKENS, 1), jnp.float32) < 0.5, -1.0, 1.0)
    base = jnp.clip(jax.random.normal(key_base, (TOKENS, D), jnp.float32), -3.5, 3.5)
    level = sign * jax.random.uniform(key_offset, (TOKENS, 1), jnp.float32, 0.5, 1.5)
    values = base * row_scale * col_scale + level * (1.0 + 2.0 * position)
    band_size = jax.random.uniform(key_band_size, (TOKENS, D), jnp.float32, 0.85, 1.2)
    band_values = band_sign * 10.0 * row_scale * band_size
    values = jnp.where(in_band[None, :], band_values, values)
    return values.astype(jnp.bfloat16)


def block_levels(stream_key, extent, pieces, low, high):
    factor_of, own = 1.0, jax.random.fold_in(stream_key, 6)
    for dim, parts in pieces:
        heights = jnp.exp(jax.random.uniform(jax.random.fold_in(own, dim), (parts,), jnp.float32, low / len(pieces), high / len(pieces)))
        factor_of = factor_of * jnp.repeat(heights, extent[dim] // parts).reshape([-1 if axis == dim else 1 for axis in range(len(extent))])
    return factor_of


def gaussian(own_key, extent, width, reach, shards=(), held_as=jnp.bfloat16):
    result = jax.random.normal(own_key, extent, jnp.float32) * width
    if len(shards) > 0:
        result = block_levels(own_key, extent, shards, -0.22, 0.18) * result
    return jnp.clip(result, min=-reach, max=reach).astype(held_as)


def setup_inputs(seed: int = 0) -> dict:
    seeds = jax.random.split(jax.random.key(seed), 8)
    return {
        "inputs": draw_inputs(jax.random.fold_in(seeds[7], 71), 0),
        "ln_gain": jnp.clip(1.0 + 0.15 * jax.random.normal(seeds[1], (D,), jnp.float32), 0.25, 1.75),
        "ln_bias": gaussian(seeds[2], (D,), 0.3, 4.0, ((0, 16),), jnp.float32),
        "w_up": gaussian(seeds[3], (D, FFW), D ** -0.5, 0.0546875, ((0, 16), (1, 32))),
        "up_bias": gaussian(seeds[4], (FFW,), 0.5, 4.0, ((0, 32),), jnp.float32),
        "w_down": gaussian(seeds[5], (FFW, D), FFW ** -0.5, 0.02734375, ((0, 32), (1, 16))),
        "down_bias": gaussian(seeds[6], (D,), 0.5, 4.0, ((0, 16),), jnp.float32),
    }


def reference(inputs, ln_gain, ln_bias, w_up, up_bias, w_down, down_bias):
    in_float = inputs.astype(jnp.float32)
    average = lax.optimization_barrier(jnp.sum(in_float, axis=1, keepdims=True)) / D
    centered = in_float - average
    variance = lax.optimization_barrier(jnp.sum(centered * centered, axis=1, keepdims=True)) / D
    normed = (centered * lax.rsqrt(variance + 1e-05) * ln_gain + ln_bias).astype(jnp.bfloat16)
    feat_block = D // N_ROW

    def up_step(accumulated, block_index):
        offset = (block_index * feat_block).astype(jnp.int32)
        left_part = lax.dynamic_slice_in_dim(normed, offset, feat_block, 1)
        right_part = lax.dynamic_slice_in_dim(w_up, offset, feat_block, 0)
        partial_value = jnp.dot(left_part, right_part, preferred_element_type=jnp.float32)
        partial_value = lax.optimization_barrier(partial_value.astype(jnp.bfloat16)).astype(jnp.float32)
        return (accumulated + partial_value, None)
    up_sum, _ = lax.scan(up_step, jnp.zeros((TOKENS, FFW), jnp.float32), jnp.arange(N_ROW, dtype=jnp.int32))
    hidden = jax.nn.gelu(up_sum + up_bias, approximate=True).astype(jnp.bfloat16)
    unit_block = FFW // N_COL

    def down_step(accumulated, block_index):
        offset = (block_index * unit_block).astype(jnp.int32)
        left_part = lax.dynamic_slice_in_dim(hidden, offset, unit_block, 1)
        right_part = lax.dynamic_slice_in_dim(w_down, offset, unit_block, 0)
        partial_value = jnp.dot(left_part, right_part, preferred_element_type=jnp.float32)
        partial_value = lax.optimization_barrier(partial_value.astype(jnp.bfloat16)).astype(jnp.float32)
        return (accumulated + partial_value, None)
    down_sum, _ = lax.scan(down_step, jnp.zeros((TOKENS, D), jnp.float32), jnp.arange(N_COL, dtype=jnp.int32))
    return (in_float + down_sum + down_bias).astype(jnp.bfloat16)
```

```python
import functools

import jax
import jax.numpy as jnp
from jax import lax
from jax.experimental import pallas as pl
from jax.experimental.pallas import tpu as pltpu
from jax.sharding import PartitionSpec as P

F32, BF16 = jnp.float32, jnp.bfloat16
MESH = pl.DeviceIdType.MESH
EPS = 1e-05
J = 4
SPLIT = ((0, 1), (2, 3))
RS_ORDER = ((2, 3, 0, 1), (0, 1, 2, 3))
AG_ORDER = ((0, 1, 2, 3), (2, 3, 0, 1))
GROUPS = 3


def kernel(
    n,
    x_ref, gain_ref, bias_ref, ub_ref, db_ref, wu_hbm, wd_hbm,
    out_ref,
    wu, wd, xg, pbuf, lm, lm2, st_out, st_in, gb, gb_in, rs_out, rs_in, ag_own, ag_in,
    tb, pair_out, pair_in, star_out, star_in,
    w_sem, x_ss, x_rs, st_ss, st_rs, gb_ss, gb_rs, r_ss, r_rs, a_ss, a_rs, p_ss, p_rs, s_ss, s_rs,
):
    half = n // 2
    feat, unit = wu.shape
    width = unit // J
    rows = 2 * GROUPS * 8
    z, c = lax.axis_index("row"), lax.axis_index("col")
    q, e = c // 2, lax.rem(c, 2)
    offs = tuple(p * (n // GROUPS) for p in range(GROUPS))
    sibling = (z, c + 1 - 2 * e)
    along = ((lax.rem(z + 1, n), c), (lax.rem(z + n - 1, n), c))
    lane = lax.broadcasted_iota(jnp.int32, (8, 128), 1)
    head = lane < 2 * GROUPS

    def remote(src, dst, ss, rs, to):
        return pltpu.make_async_remote_copy(
            src_ref=src, dst_ref=dst, send_sem=ss, recv_sem=rs, device_id=to, device_id_type=MESH
        )

    def drain(ref, sem):
        pltpu.make_async_copy(ref, ref, sem).wait()

    load_up = pltpu.make_async_copy(wu_hbm, wu, w_sem.at[0])
    load_down = pltpu.make_async_copy(wd_hbm, wd, w_sem.at[1])
    load_up.start()
    load_down.start()

    barrier = pltpu.get_barrier_semaphore()
    for to in along:
        pl.semaphore_signal(barrier, inc=1, device_id=to, device_id_type=MESH)

    def greet(i, carry):
        to = (z, lax.rem(c + i, 2 * n))
        pl.semaphore_signal(barrier, inc=1, device_id=to, device_id_type=MESH)
        return carry

    lax.fori_loop(1, 2 * n, greet, 0)
    pl.semaphore_wait(barrier, 2 * n + 1)

    def spread(far):
        for p in range(GROUPS):
            k = lax.rem(q + offs[p], n)
            dist = jnp.minimum(lax.rem(k - z + n, n), lax.rem(z - k + n, n))

            @pl.when(dist == far)
            def _():
                place = xg.at[k * 2 * GROUPS + e * GROUPS + p]
                pltpu.make_async_copy(x_ref.at[p], place, x_rs.at[k]).start()

                def send(i, carry):
                    to = (z, lax.rem(c + i, 2 * n))
                    remote(x_ref.at[p], place, x_ss, x_rs.at[k], to).start()
                    return carry

                lax.fori_loop(1, 2 * n, send, 0)

    def columns(tile):
        return jnp.concatenate([tile[:, g : g + 1][None] for g in range(2 * GROUPS)], axis=0)

    def centered(k, d):
        at = pl.ds(k * 2 * GROUPS, 2 * GROUPS)
        x = xg[at].astype(F32)
        mean = jnp.sum(x, axis=2, keepdims=True) * (1.0 / feat)
        x = x - mean
        square = jnp.sum(x * x, axis=2, keepdims=True)
        m_tile = jnp.zeros((8, 128), F32)
        s_tile = jnp.zeros((8, 128), F32)
        for g in range(2 * GROUPS):
            m_tile = jnp.where(lane == g, mean[g], m_tile)
            s_tile = jnp.where(lane == g, square[g], s_tile)
        lm[d] = m_tile
        lm2[d] = s_tile
        return (x * gain_ref[...][None]).reshape(rows, feat).astype(BF16)

    def chunk(d, s):
        return lax.rem(z + n + half - s, n) if d == 0 else lax.rem(z + half + s, n)

    def wait_inputs(k):
        drain(xg.at[pl.ds(k * 2 * GROUPS, 2 * GROUPS)], x_rs.at[k])

    def products(s):
        wait_inputs(chunk(0, s))

        @pl.when(s < half)
        def _():
            wait_inputs(chunk(1, s))

        both = jnp.concatenate([centered(chunk(0, s), 0), centered(chunk(1, s), 1)], axis=0)
        for i in range(3):
            cols = slice(i * (unit // 3), (i + 1) * (unit // 3))
            pbuf[:, cols] = jnp.dot(both, wu[:, cols], preferred_element_type=F32)

    def st_copy(d, s):
        return remote(st_out.at[d, s], st_in.at[d, s], st_ss, st_rs.at[d, s], along[d])

    def rs_copy(d, s, j):
        at = (d * half + s) * J + j
        return remote(rs_out.at[at], rs_in.at[at], r_ss, r_rs.at[d, s, j], along[d])

    def gb_copy(d, s, src):
        return remote(src, gb_in.at[d * half + s], gb_ss, gb_rs.at[d, s], along[d])

    def row_of(ref_value, first, j):
        per = width // 128
        return jnp.concatenate(
            [ref_value[first + j * per + i : first + j * per + i + 1] for i in range(per)], axis=1
        )

    per_row = unit // 128
    zero = jnp.zeros((rows, width), BF16)
    for d in range(2):
        for j in SPLIT[1 - d]:
            rs_in[d * half * J + j] = zero

    spread(half)
    spread(half - 1)
    spread(half - 2)

    load_up.wait()
    sub = lax.broadcasted_iota(jnp.int32, (16, feat), 0)
    gain, bias = gain_ref[...], bias_ref[...]
    gain_hi, bias_hi = gain.astype(BF16).astype(F32), bias.astype(BF16).astype(F32)
    lhs = jnp.where(
        sub == 0,
        gain_hi,
        jnp.where(
            sub == 1,
            gain - gain_hi,
            jnp.where(sub == 2, bias_hi, jnp.where(sub == 3, bias - bias_hi, 0.0)),
        ),
    ).astype(BF16)
    sums = jnp.dot(lhs, wu[...], preferred_element_type=F32)
    for i in range(per_row):
        cols = slice(i * 128, (i + 1) * 128)
        gb[i : i + 1] = sums[0:1, cols] + sums[1:2, cols]
        gb[per_row + i : per_row + i + 1] = sums[2:3, cols] + sums[3:4, cols]

    first = chunk(0, 0)
    wait_inputs(first)
    start = centered(first, 0)
    st_out[0, 0] = lm[0] + pltpu.roll(lm2[0], 64, 1)
    st_out[1, 0] = lm[0]
    for d in range(2):
        st_copy(d, 0).start()
    for i in range(2):
        for d in range(2):
            j = SPLIT[d][i]
            part = jnp.dot(start, wu[:, j * width : (j + 1) * width], preferred_element_type=F32)
            rs_out[d * half * J + j] = part.astype(BF16)
            rs_copy(d, 0, j).start()
    for d in range(2):
        gb_copy(d, 0, gb).start()
    products(1)

    def rs_step(s, carry):
        shift = []
        for d in range(2):
            st_copy(d, s - 1).wait_recv()
            got = st_in[d, s - 1]
            off = jnp.where(head, lm[d] - got, 0.0)
            square = jnp.where(head, lm2[d] + feat * off * off, 0.0)
            st_out[d, s] = got + pltpu.roll(off, 32, 1) + pltpu.roll(square, 64, 1)
            st_copy(d, s).start()
            shift.append(columns(off))
        own = gb[...]
        for i in range(J):
            for d in range(2):
                j = RS_ORDER[d][i]
                if i < 2:
                    pl.when(s > 1)(lambda d=d, j=j: rs_copy(d, s - 1, j).wait_recv())
                else:
                    rs_copy(d, s - 1, j).wait_recv()
                got = rs_in[(d * half + s - 1) * J + j].astype(F32).reshape(2 * GROUPS, 8, width)
                mine = pbuf[d * rows : (d + 1) * rows, j * width : (j + 1) * width]
                total = got + mine.reshape(2 * GROUPS, 8, width) + shift[d] * row_of(own, 0, j)[None]
                rs_out[(d * half + s) * J + j] = total.reshape(rows, width).astype(BF16)
                rs_copy(d, s, j).start()
        gb_copy(0, s - 1, gb).wait_recv()
        gb_copy(0, s, gb_in.at[s - 1]).start()
        gb_copy(1, s - 1, gb).wait_recv()

        @pl.when(s < half - 1)
        def _():
            gb_copy(1, s, gb_in.at[half + s - 1]).start()

        spread(half - 2 - s)
        products(s + 1)
        return carry

    lax.fori_loop(1, half, rs_step, 0)

    def ag_copy(d, s, j, src):
        at = (d * half + s) * J + j
        return remote(src, ag_in.at[at], a_ss, a_rs.at[d, s, j], along[d])

    gb_copy(0, half - 1, gb).wait_recv()
    load_down.wait()
    gb_all = gb[...]
    for i in range(2 * half - 1):
        gb_all = gb_all + gb_in[i]
    own = gb[...]
    for d in range(2):
        st_copy(d, half - 1).wait_recv()
    up, down = st_in[0, half - 1], st_in[1, half - 1]
    off = jnp.where(head, lm[0] - up, 0.0)
    mean_off = (pltpu.roll(up + down, 96, 1) + off) * (1.0 / n)
    square = pltpu.roll(up + down, 64, 1) + lm2[0] + feat * off * off
    scale = lax.rsqrt(square * (1.0 / (n * feat)) - mean_off * mean_off + EPS)
    off_c, mean_c, scale_c = columns(off), columns(mean_off), columns(scale)
    for j in range(J):
        cols = slice(j * width, (j + 1) * width)
        total = pbuf[0:rows, cols].reshape(2 * GROUPS, 8, width)
        for d in range(2):
            rs_copy(d, half - 1, j).wait_recv()
            got = rs_in[(d * half + half - 1) * J + j]
            total = total + got.astype(F32).reshape(2 * GROUPS, 8, width)
        total = total + off_c * row_of(own, 0, j)[None] - mean_c * row_of(gb_all, 0, j)[None]
        v = total * scale_c + row_of(gb_all, per_row, j)[None] + ub_ref[:, cols][None]
        hidden = jax.nn.gelu(v, approximate=True)
        ag_own[j] = hidden.reshape(rows, width).astype(BF16)
        for d in range(2):
            ag_copy(d, 0, j, ag_own.at[j]).start()

    def pair_copy(k):
        return remote(pair_out.at[k], pair_in.at[k], p_ss, p_rs.at[k], sibling)

    def to_pair(k, value):
        tb[k] = value.reshape(2 * GROUPS, 8, feat)
        pair_out[k] = tb[k, pl.ds((1 - e) * GROUPS, GROUPS)].astype(BF16)
        pair_copy(k).start()

    def to_owner(k):
        pair_copy(k).wait_recv()
        star_out[k] = (tb[k, pl.ds(e * GROUPS, GROUPS)] + pair_in[k].astype(F32)).astype(BF16)
        for p in range(GROUPS):
            owner = lax.rem(k - offs[p] + n, n)
            place = star_in.at[p * n + q]

            @pl.when(owner == q)
            def _():
                pltpu.make_async_copy(star_out.at[k, p], place, s_rs).start()

            @pl.when(owner != q)
            def _():
                remote(star_out.at[k, p], place, s_ss, s_rs, (z, 2 * owner + e)).start()

    def down_product(pieces):
        return jnp.dot(jnp.concatenate(pieces, axis=1), wd[...], preferred_element_type=F32)

    to_pair(z, down_product([ag_own[j] for j in range(J)]))

    def ag_step(s, carry):
        for i in range(J):
            for d in range(2):
                j = AG_ORDER[d][i]
                ag_copy(d, s, j, ag_own.at[j]).wait_recv()
                held = ag_in.at[(d * half + s) * J + j]
                if i < 2:
                    ag_copy(d, s + 1, j, held).start()
                else:
                    pl.when(s < half - 2)(lambda d=d, j=j, held=held: ag_copy(d, s + 1, j, held).start())
        to_owner(lax.rem(z - s + n, n))
        pl.when(s > 0)(lambda: to_owner(lax.rem(z + s, n)))
        value = down_product(
            [
                jnp.concatenate([ag_in[s * J + j], ag_in[(half + s) * J + j]], axis=0)
                for j in range(J)
            ]
        )
        to_pair(lax.rem(z - 1 - s + n, n), value[:rows])
        to_pair(lax.rem(z + 1 + s, n), value[rows:])
        return carry

    lax.fori_loop(0, half - 1, ag_step, 0)
    to_owner(lax.rem(z + 1 + half, n))
    to_owner(lax.rem(z + half - 1, n))
    pieces = []
    for d in range(2):
        for j in SPLIT[d]:
            ag_copy(d, half - 1, j, ag_own.at[j]).wait_recv()
            pieces.append(ag_in[(d * half + half - 1) * J + j])
    last = lax.rem(z + half, n)
    to_pair(last, down_product(pieces))
    to_owner(last)

    drain(star_in, s_rs)
    for p in range(GROUPS):
        total = jnp.sum(star_in[p * n : (p + 1) * n].astype(F32), axis=0)
        out_ref[p] = (x_ref[p].astype(F32) + total + db_ref[...]).astype(BF16)

    drain(xg.at[pl.ds(0, GROUPS * (2 * n - 1))], x_ss)
    drain(st_in, st_ss)
    drain(gb_in.at[pl.ds(0, n - 1)], gb_ss)
    drain(rs_in.at[pl.ds(0, (n - 1) * J)], r_ss)
    drain(ag_in.at[pl.ds(0, (n - 1) * J)], a_ss)
    drain(pair_in, p_ss)
    drain(star_in.at[pl.ds(0, GROUPS * (n - 1))], s_ss)


def local(n, inputs, ln_gain, ln_bias, w_up, up_bias, w_down, down_bias):
    feat, unit = w_up.shape
    half, rows, width = n // 2, 2 * GROUPS * 8, unit // J
    vmem, hbm = pl.BlockSpec(memory_space=pltpu.VMEM), pl.BlockSpec(memory_space=pl.ANY)
    sem = pltpu.SemaphoreType.DMA
    out = pl.pallas_call(
        functools.partial(kernel, n),
        out_shape=jax.ShapeDtypeStruct((GROUPS, 8, feat), BF16),
        in_specs=[vmem] * 5 + [hbm] * 2,
        out_specs=vmem,
        scratch_shapes=[
            pltpu.VMEM((feat, unit), BF16),
            pltpu.VMEM((unit, feat), BF16),
            pltpu.VMEM((n * 2 * GROUPS, 8, feat), BF16),
            pltpu.VMEM((2 * rows, unit), F32),
            pltpu.VMEM((2, 8, 128), F32),
            pltpu.VMEM((2, 8, 128), F32),
            pltpu.VMEM((2, half, 8, 128), F32),
            pltpu.VMEM((2, half, 8, 128), F32),
            pltpu.VMEM((2 * unit // 128, 128), F32),
            pltpu.VMEM((n, 2 * unit // 128, 128), F32),
            pltpu.VMEM((2 * half * J, rows, width), BF16),
            pltpu.VMEM((2 * half * J, rows, width), BF16),
            pltpu.VMEM((J, rows, width), BF16),
            pltpu.VMEM((2 * half * J, rows, width), BF16),
            pltpu.VMEM((n, 2 * GROUPS, 8, feat), F32),
            pltpu.VMEM((n, GROUPS, 8, feat), BF16),
            pltpu.VMEM((n, GROUPS, 8, feat), BF16),
            pltpu.VMEM((n, GROUPS, 8, feat), BF16),
            pltpu.VMEM((GROUPS * n, 8, feat), BF16),
            sem((2,)),
            sem,
            sem((n,)),
            sem,
            sem((2, half)),
            sem,
            sem((2, half)),
            sem,
            sem((2, half, J)),
            sem,
            sem((2, half, J)),
            sem,
            sem((n,)),
            sem,
            sem,
        ],
        compiler_params=pltpu.CompilerParams(
            collective_id=0, has_side_effects=True, vmem_limit_bytes=50 << 20
        ),
    )(
        inputs.reshape(GROUPS, 8, feat),
        ln_gain[None],
        ln_bias[None],
        up_bias[None],
        down_bias[None],
        w_up,
        w_down,
    )
    return out.reshape(GROUPS * 8, feat)


def solution(mesh):
    placed = (
        P("col", "row"),
        P("row"),
        P("row"),
        P("row", "col"),
        P("col"),
        P("col", "row"),
        P("row"),
    )
    return jax.shard_map(
        functools.partial(local, mesh.shape["row"]),
        mesh=mesh,
        in_specs=placed,
        out_specs=P("col", "row"),
        check_vma=False,
    )
```

```python
import functools

import jax
import jax.numpy as jnp
from jax import lax
from jax.experimental import pallas as pl
from jax.experimental.pallas import tpu as pltpu
from jax.sharding import PartitionSpec as P

F32, BF16 = jnp.float32, jnp.bfloat16
MESH = pl.DeviceIdType.MESH
EPS = 1e-05
J = 4
SPLIT = ((0, 1), (2, 3))
RS_ORDER = ((2, 0, 3, 1), (0, 2, 1, 3))
LAST_ORDER = (0, 2, 1, 3)
AG_ORDER = ((0, 2, 1, 3), (0, 2, 1, 3))
GROUPS = 3


def kernel(
    n,
    x_hbm, gain_hbm, bias_hbm, ub_hbm, db_hbm, wu_hbm, wd_hbm,
    out_ref,
    x_ref, gain_ref, bias_ref, ub_ref, db_ref, wu, wd, xg, pbuf, lm, lm2, st_out, st_in, gb_rows, gb, gb_in, rs_out, rs_in, ag_own, ag_in,
    tb, pair_out, pair_in, star_out, star_in,
    w_sem, x_ss, x_rs, f_ss, f_rs, st_ss, st_rs, gb_ss, gb_rs, r_ss, r_rs, a_ss, a_rs, p_ss, p_rs, s_ss, s_rs,
):
    half = n // 2
    feat, unit = wu.shape
    width = unit // J
    rows = 2 * GROUPS * 8
    z, c = lax.axis_index("row"), lax.axis_index("col")
    q, e = c // 2, lax.rem(c, 2)
    offs = tuple(p * (n // GROUPS) for p in range(GROUPS))
    sibling = (z, c + 1 - 2 * e)
    along = ((lax.rem(z + 1, n), c), (lax.rem(z + n - 1, n), c))
    lane = lax.broadcasted_iota(jnp.int32, (8, 128), 1)
    head = lane < 2 * GROUPS

    def remote(src, dst, ss, rs, to):
        return pltpu.make_async_remote_copy(
            src_ref=src, dst_ref=dst, send_sem=ss, recv_sem=rs, device_id=to, device_id_type=MESH
        )

    def drain(ref, sem):
        pltpu.make_async_copy(ref, ref, sem).wait()

    load_x = pltpu.make_async_copy(x_hbm, x_ref, w_sem.at[0])
    load_up = pltpu.make_async_copy(wu_hbm, wu, w_sem.at[1])
    load_down = pltpu.make_async_copy(wd_hbm, wd, w_sem.at[2])
    load_rows = [
        pltpu.make_async_copy(src, dst.at[0], w_sem.at[3 + i])
        for i, (src, dst) in enumerate(
            ((gain_hbm, gain_ref), (bias_hbm, bias_ref), (ub_hbm, ub_ref), (db_hbm, db_ref))
        )
    ]
    for load in (load_x, *load_rows, load_up, load_down):
        load.start()

    barrier = pltpu.get_barrier_semaphore()
    for to in (*along, sibling):
        pl.semaphore_signal(barrier, inc=1, device_id=to, device_id_type=MESH)

    def peer(i):
        return (z, 2 * lax.rem(q + i, n) + e)

    def greet(i, carry):
        pl.semaphore_signal(barrier, inc=1, device_id=peer(i), device_id_type=MESH)
        return carry

    lax.fori_loop(1, n, greet, 0)
    pl.semaphore_wait(barrier, n + 2)

    def spread(far):
        for p in range(GROUPS):
            k = lax.rem(q + offs[p], n)
            dist = jnp.minimum(lax.rem(k - z + n, n), lax.rem(z - k + n, n))

            @pl.when(dist == far)
            def _():
                place = xg.at[k * 2 * GROUPS + e * GROUPS + p]
                pltpu.make_async_copy(x_ref.at[p], place, x_rs.at[k]).start()

                def send(i, carry):
                    remote(x_ref.at[p], place, x_ss, x_rs.at[k], peer(i)).start()
                    return carry

                lax.fori_loop(1, n, send, 0)

    def forward(k):
        held = xg.at[pl.ds(k * 2 * GROUPS + e * GROUPS, GROUPS)]
        drain(held, x_rs.at[k])
        remote(held, held, f_ss, f_rs.at[k], sibling).start()

    def columns(tile):
        return jnp.concatenate([tile[:, g : g + 1][None] for g in range(2 * GROUPS)], axis=0)

    def centered(k, d):
        at = pl.ds(k * 2 * GROUPS, 2 * GROUPS)
        x = xg[at].astype(F32)
        mean = jnp.sum(x, axis=2, keepdims=True) * (1.0 / feat)
        x = x - mean
        square = jnp.sum(x * x, axis=2, keepdims=True)
        m_tile = jnp.zeros((8, 128), F32)
        s_tile = jnp.zeros((8, 128), F32)
        for g in range(2 * GROUPS):
            m_tile = jnp.where(lane == g, mean[g], m_tile)
            s_tile = jnp.where(lane == g, square[g], s_tile)
        lm[d] = m_tile
        lm2[d] = s_tile
        return (x * gain_ref[...][None]).reshape(rows, feat).astype(BF16)

    def chunk(d, s):
        return lax.rem(z + n + half - s, n) if d == 0 else lax.rem(z + half + s, n)

    def wait_inputs(k):
        drain(xg.at[pl.ds(k * 2 * GROUPS, GROUPS)], f_rs.at[k])

    def products(s):
        wait_inputs(chunk(0, s))

        @pl.when(s < half)
        def _():
            wait_inputs(chunk(1, s))

        both = jnp.concatenate([centered(chunk(0, s), 0), centered(chunk(1, s), 1)], axis=0)
        for i in range(3):
            cols = slice(i * (unit // 3), (i + 1) * (unit // 3))
            pbuf[:, cols] = jnp.dot(both, wu[:, cols], preferred_element_type=F32)

    def st_copy(d, s):
        return remote(st_out.at[d, s], st_in.at[d, s], st_ss, st_rs.at[d, s], along[d])

    def rs_copy(d, s, j):
        at = (d * half + s) * J + j
        return remote(rs_out.at[at], rs_in.at[at], r_ss, r_rs.at[d, s, j], along[d])

    def gb_copy(d, s, src):
        return remote(src, gb_in.at[d * half + s], gb_ss, gb_rs.at[d, s], along[d])

    def row_of(ref_value, first, j):
        per = width // 128
        return jnp.concatenate(
            [ref_value[first + j * per + i : first + j * per + i + 1] for i in range(per)], axis=1
        )

    per_row = unit // 128
    gb_rows[...] = jnp.zeros_like(gb_rows)
    zero = jnp.zeros((rows, width), BF16)
    for d in range(2):
        for j in SPLIT[1 - d]:
            rs_in[d * half * J + j] = zero

    load_x.wait()
    def spread_all(i, carry):
        spread(half - i)
        return carry

    lax.fori_loop(0, half + 1, spread_all, 0)

    for load in load_rows:
        load.wait()
    load_up.wait()
    first = chunk(0, 0)
    forward(first)
    wait_inputs(first)
    start = centered(first, 0)
    st_out[0, 0] = lm[0] + pltpu.roll(lm2[0], 64, 1)
    st_out[1, 0] = lm[0]
    for d in range(2):
        st_copy(d, 0).start()
    for i in range(2):
        for d in range(2):
            j = SPLIT[d][i]
            part = jnp.dot(start, wu[:, j * width : (j + 1) * width], preferred_element_type=F32)
            rs_out[d * half * J + j] = part.astype(BF16)
            rs_copy(d, 0, j).start()
    for s in (1, 2):
        for d in range(2):
            forward(chunk(d, s))
    sub = lax.broadcasted_iota(jnp.int32, (16, feat), 0)
    gain, bias = gain_ref[...], bias_ref[...]
    gain_hi, bias_hi = gain.astype(BF16).astype(F32), bias.astype(BF16).astype(F32)
    lhs = jnp.where(
        sub == 0,
        gain_hi,
        jnp.where(
            sub == 1,
            gain - gain_hi,
            jnp.where(sub == 2, bias_hi, jnp.where(sub == 3, bias - bias_hi, 0.0)),
        ),
    ).astype(BF16)
    sums = jnp.dot(lhs, wu[...], preferred_element_type=F32)
    for i in range(per_row):
        cols = slice(i * 128, (i + 1) * 128)
        gb_rows[i : i + 1] = sums[0:1, cols] + sums[1:2, cols]
        gb_rows[per_row + i : per_row + i + 1] = sums[2:3, cols] + sums[3:4, cols]
    gb[...] = gb_rows[...].astype(BF16)
    for d in range(2):
        gb_copy(d, 0, gb).start()
    products(1)

    def rs_step(s, carry):
        shift = []
        for d in range(2):
            st_copy(d, s - 1).wait_recv()
            got = st_in[d, s - 1]
            off = jnp.where(head, lm[d] - got, 0.0)
            square = jnp.where(head, lm2[d] + feat * off * off, 0.0)
            st_out[d, s] = got + pltpu.roll(off, 32, 1) + pltpu.roll(square, 64, 1)
            st_copy(d, s).start()
            shift.append(columns(off))
        own = gb_rows[...]
        for i in range(J):
            for d in range(2):
                j = RS_ORDER[d][i]
                if j in SPLIT[1 - d]:
                    pl.when(s > 1)(lambda d=d, j=j: rs_copy(d, s - 1, j).wait_recv())
                else:
                    rs_copy(d, s - 1, j).wait_recv()
                got = rs_in[(d * half + s - 1) * J + j].astype(F32).reshape(2 * GROUPS, 8, width)
                mine = pbuf[d * rows : (d + 1) * rows, j * width : (j + 1) * width]
                total = got + mine.reshape(2 * GROUPS, 8, width) + shift[d] * row_of(own, 0, j)[None]
                rs_out[(d * half + s) * J + j] = total.reshape(rows, width).astype(BF16)
                rs_copy(d, s, j).start()
        gb_copy(0, s - 1, gb).wait_recv()
        gb_copy(0, s, gb_in.at[s - 1]).start()
        gb_copy(1, s - 1, gb).wait_recv()

        @pl.when(s < half - 1)
        def _():
            gb_copy(1, s, gb_in.at[half + s - 1]).start()

        pl.when(s < half - 1)(lambda: forward(chunk(0, s + 2)))
        pl.when(s < half - 2)(lambda: forward(chunk(1, s + 2)))
        products(s + 1)
        return carry

    lax.fori_loop(1, half, rs_step, 0)

    def ag_copy(d, s, j, src):
        at = (d * half + s) * J + j
        return remote(src, ag_in.at[at], a_ss, a_rs.at[d, s, j], along[d])

    gb_copy(0, half - 1, gb).wait_recv()
    load_down.wait()
    own = gb_rows[...]
    gb_all = own
    for i in range(2 * half - 1):
        gb_all = gb_all + gb_in[i].astype(F32)
    for d in range(2):
        st_copy(d, half - 1).wait_recv()
    up, down = st_in[0, half - 1], st_in[1, half - 1]
    off = jnp.where(head, lm[0] - up, 0.0)
    mean_off = (pltpu.roll(up + down, 96, 1) + off) * (1.0 / n)
    square = pltpu.roll(up + down, 64, 1) + lm2[0] + feat * off * off
    scale = lax.rsqrt(square * (1.0 / (n * feat)) - mean_off * mean_off + EPS)
    off_c, mean_c, scale_c = columns(off), columns(mean_off), columns(scale)
    for j in LAST_ORDER:
        cols = slice(j * width, (j + 1) * width)
        total = pbuf[0:rows, cols].reshape(2 * GROUPS, 8, width)
        for d in range(2):
            rs_copy(d, half - 1, j).wait_recv()
            got = rs_in[(d * half + half - 1) * J + j]
            total = total + got.astype(F32).reshape(2 * GROUPS, 8, width)
        total = total + off_c * row_of(own, 0, j)[None] - mean_c * row_of(gb_all, 0, j)[None]
        v = total * scale_c + row_of(gb_all, per_row, j)[None] + ub_ref[:, cols][None]
        hidden = jax.nn.gelu(v, approximate=True)
        ag_own[j] = hidden.reshape(rows, width).astype(BF16)
        for d in range(2):
            ag_copy(d, 0, j, ag_own.at[j]).start()

    def pair_copy(k):
        return remote(pair_out.at[k], pair_in.at[k], p_ss, p_rs.at[k], sibling)

    def to_pair(k, value):
        tb[k] = value.reshape(2 * GROUPS, 8, feat)
        pair_out[k] = tb[k, pl.ds((1 - e) * GROUPS, GROUPS)].astype(BF16)
        pair_copy(k).start()

    def to_owner(k):
        pair_copy(k).wait_recv()
        star_out[k] = (tb[k, pl.ds(e * GROUPS, GROUPS)] + pair_in[k].astype(F32)).astype(BF16)
        for p in range(GROUPS):
            owner = lax.rem(k - offs[p] + n, n)
            place = star_in.at[p * n + q]

            @pl.when(owner == q)
            def _():
                pltpu.make_async_copy(star_out.at[k, p], place, s_rs).start()

            @pl.when(owner != q)
            def _():
                remote(star_out.at[k, p], place, s_ss, s_rs, (z, 2 * owner + e)).start()

    def down_product(pieces):
        return jnp.dot(jnp.concatenate(pieces, axis=1), wd[...], preferred_element_type=F32)

    to_pair(z, down_product([ag_own[j] for j in range(J)]))

    def ag_step(s, carry):
        for i in range(J):
            for d in range(2):
                j = AG_ORDER[d][i]
                ag_copy(d, s, j, ag_own.at[j]).wait_recv()
                held = ag_in.at[(d * half + s) * J + j]
                if j in SPLIT[d]:
                    ag_copy(d, s + 1, j, held).start()
                else:
                    pl.when(s < half - 2)(lambda d=d, j=j, held=held: ag_copy(d, s + 1, j, held).start())
        to_owner(lax.rem(z - s + n, n))
        pl.when(s > 0)(lambda: to_owner(lax.rem(z + s, n)))
        value = down_product(
            [
                jnp.concatenate([ag_in[s * J + j], ag_in[(half + s) * J + j]], axis=0)
                for j in range(J)
            ]
        )
        to_pair(lax.rem(z - 1 - s + n, n), value[:rows])
        to_pair(lax.rem(z + 1 + s, n), value[rows:])
        return carry

    lax.fori_loop(0, half - 1, ag_step, 0)
    to_owner(lax.rem(z + 1 + half, n))
    to_owner(lax.rem(z + half - 1, n))
    pieces = []
    for d in range(2):
        for j in SPLIT[d]:
            ag_copy(d, half - 1, j, ag_own.at[j]).wait_recv()
            pieces.append(ag_in[(d * half + half - 1) * J + j])
    last = lax.rem(z + half, n)
    to_pair(last, down_product(pieces))
    to_owner(last)

    drain(star_in, s_rs)
    for p in range(GROUPS):
        total = jnp.sum(star_in[p * n : (p + 1) * n].astype(F32), axis=0)
        out_ref[p] = (x_ref[p].astype(F32) + total + db_ref[...]).astype(BF16)

    drain(xg.at[pl.ds(0, GROUPS * (n - 1))], x_ss)
    drain(xg.at[pl.ds(0, GROUPS * n)], f_ss)
    drain(st_in, st_ss)
    drain(gb_in.at[pl.ds(0, n - 1)], gb_ss)
    drain(rs_in.at[pl.ds(0, (n - 1) * J)], r_ss)
    drain(ag_in.at[pl.ds(0, (n - 1) * J)], a_ss)
    drain(pair_in, p_ss)
    drain(star_in.at[pl.ds(0, GROUPS * (n - 1))], s_ss)


def local(n, inputs, ln_gain, ln_bias, w_up, up_bias, w_down, down_bias):
    feat, unit = w_up.shape
    half, rows, width = n // 2, 2 * GROUPS * 8, unit // J
    tall = (2 * unit // 128 + 15) // 16 * 16
    vmem, hbm = pl.BlockSpec(memory_space=pltpu.VMEM), pl.BlockSpec(memory_space=pltpu.HBM)
    sem = pltpu.SemaphoreType.DMA
    out = pl.pallas_call(
        functools.partial(kernel, n),
        out_shape=jax.ShapeDtypeStruct((GROUPS, 8, feat), BF16),
        in_specs=[hbm] * 7,
        out_specs=vmem,
        scratch_shapes=[
            pltpu.VMEM((GROUPS, 8, feat), BF16),
            pltpu.VMEM((1, feat), F32),
            pltpu.VMEM((1, feat), F32),
            pltpu.VMEM((1, unit), F32),
            pltpu.VMEM((1, feat), F32),
            pltpu.VMEM((feat, unit), BF16),
            pltpu.VMEM((unit, feat), BF16),
            pltpu.VMEM((n * 2 * GROUPS, 8, feat), BF16),
            pltpu.VMEM((2 * rows, unit), F32),
            pltpu.VMEM((2, 8, 128), F32),
            pltpu.VMEM((2, 8, 128), F32),
            pltpu.VMEM((2, half, 8, 128), F32),
            pltpu.VMEM((2, half, 8, 128), F32),
            pltpu.VMEM((tall, 128), F32),
            pltpu.VMEM((tall, 128), BF16),
            pltpu.VMEM((n, tall, 128), BF16),
            pltpu.VMEM((2 * half * J, rows, width), BF16),
            pltpu.VMEM((2 * half * J, rows, width), BF16),
            pltpu.VMEM((J, rows, width), BF16),
            pltpu.VMEM((2 * half * J, rows, width), BF16),
            pltpu.VMEM((n, 2 * GROUPS, 8, feat), F32),
            pltpu.VMEM((n, GROUPS, 8, feat), BF16),
            pltpu.VMEM((n, GROUPS, 8, feat), BF16),
            pltpu.VMEM((n, GROUPS, 8, feat), BF16),
            pltpu.VMEM((GROUPS * n, 8, feat), BF16),
            sem((7,)),
            sem,
            sem((n,)),
            sem,
            sem((n,)),
            sem,
            sem((2, half)),
            sem,
            sem((2, half)),
            sem,
            sem((2, half, J)),
            sem,
            sem((2, half, J)),
            sem,
            sem((n,)),
            sem,
            sem,
        ],
        compiler_params=pltpu.CompilerParams(
            collective_id=0, has_side_effects=True, vmem_limit_bytes=50 << 20
        ),
    )(
        *(
            pltpu.with_memory_space_constraint(a, pltpu.HBM)
            for a in (
                inputs.reshape(GROUPS, 8, feat),
                ln_gain,
                ln_bias,
                up_bias,
                down_bias,
                w_up,
                w_down,
            )
        )
    )
    return out.reshape(GROUPS * 8, feat)


def solution(mesh):
    placed = (
        P("col", "row"),
        P("row"),
        P("row"),
        P("row", "col"),
        P("col"),
        P("col", "row"),
        P("row"),
    )
    return jax.shard_map(
        functools.partial(local, mesh.shape["row"]),
        mesh=mesh,
        in_specs=placed,
        out_specs=P("col", "row"),
        check_vma=False,
    )
```

```python
import functools

import jax
import jax.numpy as jnp
from jax import lax
from jax.experimental import pallas as pl
from jax.experimental.pallas import tpu as pltpu
from jax.sharding import PartitionSpec as P

F32, BF16 = jnp.float32, jnp.bfloat16
MESH = pl.DeviceIdType.MESH
EPS = 1e-05
J = 4
SPLIT = ((0, 1), (2, 3))
RS_ORDER = ((2, 0, 3, 1), (0, 2, 1, 3))
LAST_ORDER = (0, 2, 1, 3)
AG_ORDER = ((0, 2, 1, 3), (0, 2, 1, 3))
FAR_FIRST = (10, 9, 11, 6, 14, 8, 2, 5, 7, 13, 15, 1, 3, 4, 12)
GROUPS = 3


def kernel(
    n,
    x_hbm, gain_hbm, bias_hbm, ub_hbm, db_hbm, wu_hbm, wd_hbm,
    out_ref,
    x_ref, gain_ref, bias_ref, ub_ref, db_ref, wu, wd, xg, pbuf, lm, lm2, st_out, st_in, gb_rows, gb, gb_in, rs_out, rs_in, ag_own, ag_in,
    tb, pair_out, pair_in, star_out, star_in,
    w_sem, x_ss, x_rs, f_ss, f_rs, st_ss, st_rs, gb_ss, gb_rs, r_ss, r_rs, a_ss, a_rs, p_ss, p_rs, s_ss, s_rs,
):
    half = n // 2
    feat, unit = wu.shape
    width = unit // J
    rows = 2 * GROUPS * 8
    z, c = lax.axis_index("row"), lax.axis_index("col")
    q, e = c // 2, lax.rem(c, 2)
    offs = tuple(p * (n // GROUPS) for p in range(GROUPS))
    sibling = (z, c + 1 - 2 * e)
    along = ((lax.rem(z + 1, n), c), (lax.rem(z + n - 1, n), c))
    lane = lax.broadcasted_iota(jnp.int32, (8, 128), 1)
    head = lane < 2 * GROUPS

    def remote(src, dst, ss, rs, to):
        return pltpu.make_async_remote_copy(
            src_ref=src, dst_ref=dst, send_sem=ss, recv_sem=rs, device_id=to, device_id_type=MESH
        )

    def drain(ref, sem):
        pltpu.make_async_copy(ref, ref, sem).wait()

    load_x = pltpu.make_async_copy(x_hbm, x_ref, w_sem.at[0])
    load_up = pltpu.make_async_copy(wu_hbm, wu, w_sem.at[1])
    load_down = pltpu.make_async_copy(wd_hbm, wd, w_sem.at[2])
    load_rows = [
        pltpu.make_async_copy(src, dst.at[0], w_sem.at[3 + i])
        for i, (src, dst) in enumerate(
            ((gain_hbm, gain_ref), (bias_hbm, bias_ref), (ub_hbm, ub_ref), (db_hbm, db_ref))
        )
    ]
    for load in (load_x, *load_rows, load_up, load_down):
        load.start()

    barrier = pltpu.get_barrier_semaphore()
    for to in (*along, sibling):
        pl.semaphore_signal(barrier, inc=1, device_id=to, device_id_type=MESH)

    def peer(i):
        return (z, 2 * lax.bitwise_xor(q, i) + e)

    def greet(i, carry):
        pl.semaphore_signal(barrier, inc=1, device_id=peer(i), device_id_type=MESH)
        return carry

    lax.fori_loop(1, n, greet, 0)
    pl.semaphore_wait(barrier, n + 2)

    def spread(far):
        for p in range(GROUPS):
            k = lax.rem(q + offs[p], n)
            dist = jnp.minimum(lax.rem(k - z + n, n), lax.rem(z - k + n, n))

            @pl.when(dist == far)
            def _():
                place = xg.at[k * 2 * GROUPS + e * GROUPS + p]
                pltpu.make_async_copy(x_ref.at[p], place, x_rs.at[k]).start()

                for i in FAR_FIRST:
                    remote(x_ref.at[p], place, x_ss, x_rs.at[k], peer(i)).start()

    def forward(k):
        held = xg.at[pl.ds(k * 2 * GROUPS + e * GROUPS, GROUPS)]
        drain(held, x_rs.at[k])
        remote(held, held, f_ss, f_rs.at[k], sibling).start()

    def columns(tile):
        return jnp.concatenate([tile[:, g : g + 1][None] for g in range(2 * GROUPS)], axis=0)

    def centered(k, d):
        at = pl.ds(k * 2 * GROUPS, 2 * GROUPS)
        x = xg[at].astype(F32)
        mean = jnp.sum(x, axis=2, keepdims=True) * (1.0 / feat)
        x = x - mean
        square = jnp.sum(x * x, axis=2, keepdims=True)
        m_tile = jnp.zeros((8, 128), F32)
        s_tile = jnp.zeros((8, 128), F32)
        for g in range(2 * GROUPS):
            m_tile = jnp.where(lane == g, mean[g], m_tile)
            s_tile = jnp.where(lane == g, square[g], s_tile)
        lm[d] = m_tile
        lm2[d] = s_tile
        return (x * gain_ref[...][None]).reshape(rows, feat).astype(BF16)

    def chunk(d, s):
        return lax.rem(z + n + half - s, n) if d == 0 else lax.rem(z + half + s, n)

    def wait_inputs(k):
        drain(xg.at[pl.ds(k * 2 * GROUPS, GROUPS)], f_rs.at[k])

    def products(s):
        wait_inputs(chunk(0, s))

        @pl.when(s < half)
        def _():
            wait_inputs(chunk(1, s))

        both = jnp.concatenate([centered(chunk(0, s), 0), centered(chunk(1, s), 1)], axis=0)
        for i in range(3):
            cols = slice(i * (unit // 3), (i + 1) * (unit // 3))
            pbuf[:, cols] = jnp.dot(both, wu[:, cols], preferred_element_type=F32)

    def st_copy(d, s):
        return remote(st_out.at[d, s], st_in.at[d, s], st_ss, st_rs.at[d, s], along[d])

    def rs_copy(d, s, j):
        at = (d * half + s) * J + j
        return remote(rs_out.at[at], rs_in.at[at], r_ss, r_rs.at[d, s, j], along[d])

    def gb_copy(d, s, src):
        return remote(src, gb_in.at[d * half + s], gb_ss, gb_rs.at[d, s], along[d])

    def row_of(ref_value, first, j):
        per = width // 128
        return jnp.concatenate(
            [ref_value[first + j * per + i : first + j * per + i + 1] for i in range(per)], axis=1
        )

    per_row = unit // 128
    gb_rows[...] = jnp.zeros_like(gb_rows)
    zero = jnp.zeros((rows, width), BF16)
    for d in range(2):
        for j in SPLIT[1 - d]:
            rs_in[d * half * J + j] = zero

    load_x.wait()
    def spread_all(i, carry):
        spread(half - i)
        return carry

    lax.fori_loop(0, half + 1, spread_all, 0)

    for load in load_rows:
        load.wait()
    load_up.wait()
    first = chunk(0, 0)
    forward(first)
    wait_inputs(first)
    start = centered(first, 0)
    st_out[0, 0] = lm[0] + pltpu.roll(lm2[0], 64, 1)
    st_out[1, 0] = lm[0]
    for d in range(2):
        st_copy(d, 0).start()
    for i in range(2):
        for d in range(2):
            j = SPLIT[d][i]
            part = jnp.dot(start, wu[:, j * width : (j + 1) * width], preferred_element_type=F32)
            rs_out[d * half * J + j] = part.astype(BF16)
            rs_copy(d, 0, j).start()
    for s in (1, 2):
        for d in range(2):
            forward(chunk(d, s))
    sub = lax.broadcasted_iota(jnp.int32, (16, feat), 0)
    gain, bias = gain_ref[...], bias_ref[...]
    gain_hi, bias_hi = gain.astype(BF16).astype(F32), bias.astype(BF16).astype(F32)
    lhs = jnp.where(
        sub == 0,
        gain_hi,
        jnp.where(
            sub == 1,
            gain - gain_hi,
            jnp.where(sub == 2, bias_hi, jnp.where(sub == 3, bias - bias_hi, 0.0)),
        ),
    ).astype(BF16)
    sums = jnp.dot(lhs, wu[...], preferred_element_type=F32)
    for i in range(per_row):
        cols = slice(i * 128, (i + 1) * 128)
        gb_rows[i : i + 1] = sums[0:1, cols] + sums[1:2, cols]
        gb_rows[per_row + i : per_row + i + 1] = sums[2:3, cols] + sums[3:4, cols]
    gb[...] = gb_rows[...].astype(BF16)
    for d in range(2):
        gb_copy(d, 0, gb).start()
    own_row = jnp.concatenate([gb_rows[i : i + 1] for i in range(per_row)], axis=1)

    def shifted(s):
        for d in range(2):
            st_copy(d, s - 1).wait_recv()
            got = st_in[d, s - 1]
            off = jnp.where(head, lm[d] - got, 0.0)

            @pl.when(s < half)
            def _():
                square = jnp.where(head, lm2[d] + feat * off * off, 0.0)
                st_out[d, s] = got + pltpu.roll(off, 32, 1) + pltpu.roll(square, 64, 1)
                st_copy(d, s).start()

            off_c = columns(off)
            for j in range(J):
                cols = slice(j * width, (j + 1) * width)
                at = slice(d * rows, (d + 1) * rows)
                mine = pbuf[at, cols].reshape(2 * GROUPS, 8, width) + off_c * own_row[:, cols][None]
                pbuf[at, cols] = mine.reshape(rows, width)

    products(1)
    shifted(1)

    def rs_step(s, carry):
        for i in range(J):
            for d in range(2):
                j = RS_ORDER[d][i]
                if j in SPLIT[1 - d]:
                    pl.when(s > 1)(lambda d=d, j=j: rs_copy(d, s - 1, j).wait_recv())
                else:
                    rs_copy(d, s - 1, j).wait_recv()
                got = rs_in[(d * half + s - 1) * J + j].astype(F32).reshape(2 * GROUPS, 8, width)
                mine = pbuf[d * rows : (d + 1) * rows, j * width : (j + 1) * width]
                total = got + mine.reshape(2 * GROUPS, 8, width)
                rs_out[(d * half + s) * J + j] = total.reshape(rows, width).astype(BF16)
                rs_copy(d, s, j).start()
        gb_copy(0, s - 1, gb).wait_recv()
        gb_copy(0, s, gb_in.at[s - 1]).start()
        gb_copy(1, s - 1, gb).wait_recv()

        @pl.when(s < half - 1)
        def _():
            gb_copy(1, s, gb_in.at[half + s - 1]).start()

        pl.when(s < half - 1)(lambda: forward(chunk(0, s + 2)))
        pl.when(s < half - 2)(lambda: forward(chunk(1, s + 2)))
        products(s + 1)
        shifted(s + 1)
        return carry

    lax.fori_loop(1, half, rs_step, 0)

    def ag_copy(d, s, j, src):
        at = (d * half + s) * J + j
        return remote(src, ag_in.at[at], a_ss, a_rs.at[d, s, j], along[d])

    gb_copy(0, half - 1, gb).wait_recv()
    load_down.wait()
    gb_all = gb_rows[...]
    for i in range(2 * half - 1):
        gb_all = gb_all + gb_in[i].astype(F32)
    up, down = st_in[0, half - 1], st_in[1, half - 1]
    off = jnp.where(head, lm[0] - up, 0.0)
    mean_off = (pltpu.roll(up + down, 96, 1) + off) * (1.0 / n)
    square = pltpu.roll(up + down, 64, 1) + lm2[0] + feat * off * off
    scale = lax.rsqrt(square * (1.0 / (n * feat)) - mean_off * mean_off + EPS)
    mean_c, scale_c = columns(mean_off), columns(scale)
    for j in LAST_ORDER:
        cols = slice(j * width, (j + 1) * width)
        total = pbuf[0:rows, cols].reshape(2 * GROUPS, 8, width)
        for d in range(2):
            rs_copy(d, half - 1, j).wait_recv()
            got = rs_in[(d * half + half - 1) * J + j]
            total = total + got.astype(F32).reshape(2 * GROUPS, 8, width)
        total = total - mean_c * row_of(gb_all, 0, j)[None]
        v = total * scale_c + row_of(gb_all, per_row, j)[None] + ub_ref[:, cols][None]
        hidden = jax.nn.gelu(v, approximate=True)
        ag_own[j] = hidden.reshape(rows, width).astype(BF16)
        for d in range(2):
            ag_copy(d, 0, j, ag_own.at[j]).start()

    def pair_copy(k):
        return remote(pair_out.at[k], pair_in.at[k], p_ss, p_rs.at[k], sibling)

    def to_pair(k, value):
        tb[k] = value.reshape(2 * GROUPS, 8, feat)
        pair_out[k] = tb[k, pl.ds((1 - e) * GROUPS, GROUPS)].astype(BF16)
        pair_copy(k).start()

    def to_owner(k):
        pair_copy(k).wait_recv()
        star_out[k] = (tb[k, pl.ds(e * GROUPS, GROUPS)] + pair_in[k].astype(F32)).astype(BF16)
        for p in range(GROUPS):
            owner = lax.rem(k - offs[p] + n, n)
            place = star_in.at[p * n + q]

            @pl.when(owner == q)
            def _():
                pltpu.make_async_copy(star_out.at[k, p], place, s_rs).start()

            @pl.when(owner != q)
            def _():
                remote(star_out.at[k, p], place, s_ss, s_rs, (z, 2 * owner + e)).start()

    def down_product(pieces):
        return jnp.dot(jnp.concatenate(pieces, axis=1), wd[...], preferred_element_type=F32)

    to_pair(z, down_product([ag_own[j] for j in range(J)]))

    def ag_step(s, carry):
        for i in range(J):
            for d in range(2):
                j = AG_ORDER[d][i]
                ag_copy(d, s, j, ag_own.at[j]).wait_recv()
                held = ag_in.at[(d * half + s) * J + j]
                if j in SPLIT[d]:
                    ag_copy(d, s + 1, j, held).start()
                else:
                    pl.when(s < half - 2)(lambda d=d, j=j, held=held: ag_copy(d, s + 1, j, held).start())
        to_owner(lax.rem(z - s + n, n))
        pl.when(s > 0)(lambda: to_owner(lax.rem(z + s, n)))
        value = down_product(
            [
                jnp.concatenate([ag_in[s * J + j], ag_in[(half + s) * J + j]], axis=0)
                for j in range(J)
            ]
        )
        to_pair(lax.rem(z - 1 - s + n, n), value[:rows])
        to_pair(lax.rem(z + 1 + s, n), value[rows:])
        return carry

    lax.fori_loop(0, half - 1, ag_step, 0)
    to_owner(lax.rem(z + 1 + half, n))
    to_owner(lax.rem(z + half - 1, n))
    pieces = []
    for d in range(2):
        for j in SPLIT[d]:
            ag_copy(d, half - 1, j, ag_own.at[j]).wait_recv()
            pieces.append(ag_in[(d * half + half - 1) * J + j])
    last = lax.rem(z + half, n)
    to_pair(last, down_product(pieces))
    to_owner(last)

    drain(star_in, s_rs)
    for p in range(GROUPS):
        total = jnp.sum(star_in[p * n : (p + 1) * n].astype(F32), axis=0)
        out_ref[p] = (x_ref[p].astype(F32) + total + db_ref[...]).astype(BF16)

    drain(xg.at[pl.ds(0, GROUPS * (n - 1))], x_ss)
    drain(xg.at[pl.ds(0, GROUPS * n)], f_ss)
    drain(st_in, st_ss)
    drain(gb_in.at[pl.ds(0, n - 1)], gb_ss)
    drain(rs_in.at[pl.ds(0, (n - 1) * J)], r_ss)
    drain(ag_in.at[pl.ds(0, (n - 1) * J)], a_ss)
    drain(pair_in, p_ss)
    drain(star_in.at[pl.ds(0, GROUPS * (n - 1))], s_ss)


def local(n, inputs, ln_gain, ln_bias, w_up, up_bias, w_down, down_bias):
    feat, unit = w_up.shape
    half, rows, width = n // 2, 2 * GROUPS * 8, unit // J
    tall = (2 * unit // 128 + 15) // 16 * 16
    vmem, hbm = pl.BlockSpec(memory_space=pltpu.VMEM), pl.BlockSpec(memory_space=pltpu.HBM)
    sem = pltpu.SemaphoreType.DMA
    out = pl.pallas_call(
        functools.partial(kernel, n),
        out_shape=jax.ShapeDtypeStruct((GROUPS, 8, feat), BF16),
        in_specs=[hbm] * 7,
        out_specs=vmem,
        scratch_shapes=[
            pltpu.VMEM((GROUPS, 8, feat), BF16),
            pltpu.VMEM((1, feat), F32),
            pltpu.VMEM((1, feat), F32),
            pltpu.VMEM((1, unit), F32),
            pltpu.VMEM((1, feat), F32),
            pltpu.VMEM((feat, unit), BF16),
            pltpu.VMEM((unit, feat), BF16),
            pltpu.VMEM((n * 2 * GROUPS, 8, feat), BF16),
            pltpu.VMEM((2 * rows, unit), F32),
            pltpu.VMEM((2, 8, 128), F32),
            pltpu.VMEM((2, 8, 128), F32),
            pltpu.VMEM((2, half, 8, 128), F32),
            pltpu.VMEM((2, half, 8, 128), F32),
            pltpu.VMEM((tall, 128), F32),
            pltpu.VMEM((tall, 128), BF16),
            pltpu.VMEM((n, tall, 128), BF16),
            pltpu.VMEM((2 * half * J, rows, width), BF16),
            pltpu.VMEM((2 * half * J, rows, width), BF16),
            pltpu.VMEM((J, rows, width), BF16),
            pltpu.VMEM((2 * half * J, rows, width), BF16),
            pltpu.VMEM((n, 2 * GROUPS, 8, feat), F32),
            pltpu.VMEM((n, GROUPS, 8, feat), BF16),
            pltpu.VMEM((n, GROUPS, 8, feat), BF16),
            pltpu.VMEM((n, GROUPS, 8, feat), BF16),
            pltpu.VMEM((GROUPS * n, 8, feat), BF16),
            sem((7,)),
            sem,
            sem((n,)),
            sem,
            sem((n,)),
            sem,
            sem((2, half)),
            sem,
            sem((2, half)),
            sem,
            sem((2, half, J)),
            sem,
            sem((2, half, J)),
            sem,
            sem((n,)),
            sem,
            sem,
        ],
        compiler_params=pltpu.CompilerParams(
            collective_id=0, has_side_effects=True, vmem_limit_bytes=50 << 20
        ),
    )(
        *(
            pltpu.with_memory_space_constraint(a, pltpu.HBM)
            for a in (
                inputs.reshape(GROUPS, 8, feat),
                ln_gain,
                ln_bias,
                up_bias,
                down_bias,
                w_up,
                w_down,
            )
        )
    )
    return out.reshape(GROUPS * 8, feat)


def solution(mesh):
    placed = (
        P("col", "row"),
        P("row"),
        P("row"),
        P("row", "col"),
        P("col"),
        P("col", "row"),
        P("row"),
    )
    return jax.shard_map(
        functools.partial(local, mesh.shape["row"]),
        mesh=mesh,
        in_specs=placed,
        out_specs=P("col", "row"),
        check_vma=False,
    )
```

```python
import functools

import jax
import jax.numpy as jnp
from jax import lax
from jax.experimental import pallas as pl
from jax.experimental.pallas import tpu as pltpu
from jax.sharding import PartitionSpec as P

F32, BF16 = jnp.float32, jnp.bfloat16
MESH = pl.DeviceIdType.MESH
EPS = 1e-05
J = 4
SPLIT = ((0, 1), (2, 3))
RS_ORDER = ((2, 0, 3, 1), (0, 2, 1, 3))
LAST_ORDER = (0, 2, 1, 3)
AG_ORDER = ((0, 2, 1, 3), (0, 2, 1, 3))
FAR_FIRST = (10, 9, 11, 6, 14, 8, 2, 5, 7, 13, 15, 1, 3, 4, 12)
GROUPS = 3


def kernel(
    n,
    x_hbm, gain_hbm, bias_hbm, ub_hbm, db_hbm, wu_hbm, wd_hbm,
    out_ref,
    x_ref, gain_ref, bias_ref, ub_ref, db_ref, wu, wd, xg, pbuf, lm, lm2, st_out, st_in, gb_rows, gb, gb_in, rs_out, rs_in, ag_own, ag_in,
    tb, pair_out, pair_in, star_out, star_in,
    w_sem, x_ss, x_rs, f_ss, f_rs, st_ss, st_rs, gb_ss, gb_rs, r_ss, r_rs, a_ss, a_rs, p_ss, p_rs, s_ss, s_rs,
):
    half = n // 2
    feat, unit = wu.shape
    width = unit // J
    rows = 2 * GROUPS * 8
    z, c = lax.axis_index("row"), lax.axis_index("col")
    q, e = c // 2, lax.rem(c, 2)
    offs = tuple(p * (n // GROUPS) for p in range(GROUPS))
    sibling = (z, c + 1 - 2 * e)
    along = ((lax.rem(z + 1, n), c), (lax.rem(z + n - 1, n), c))
    lane = lax.broadcasted_iota(jnp.int32, (8, 128), 1)
    head = lane < 2 * GROUPS

    def remote(src, dst, ss, rs, to):
        return pltpu.make_async_remote_copy(
            src_ref=src, dst_ref=dst, send_sem=ss, recv_sem=rs, device_id=to, device_id_type=MESH
        )

    def drain(ref, sem):
        pltpu.make_async_copy(ref, ref, sem).wait()

    load_x = pltpu.make_async_copy(x_hbm, x_ref, w_sem.at[0])
    load_up = pltpu.make_async_copy(wu_hbm, wu, w_sem.at[1])
    load_down = pltpu.make_async_copy(wd_hbm, wd, w_sem.at[2])
    load_rows = [
        pltpu.make_async_copy(src, dst.at[0], w_sem.at[3 + i])
        for i, (src, dst) in enumerate(
            ((gain_hbm, gain_ref), (bias_hbm, bias_ref), (ub_hbm, ub_ref), (db_hbm, db_ref))
        )
    ]
    for load in (load_x, *load_rows, load_up, load_down):
        load.start()

    barrier = pltpu.get_barrier_semaphore()
    for to in (*along, sibling):
        pl.semaphore_signal(barrier, inc=1, device_id=to, device_id_type=MESH)

    def peer(i):
        return (z, 2 * lax.bitwise_xor(q, i) + e)

    def greet(i, carry):
        pl.semaphore_signal(barrier, inc=1, device_id=peer(i), device_id_type=MESH)
        return carry

    lax.fori_loop(1, n, greet, 0)
    pl.semaphore_wait(barrier, n + 2)

    def spread(far):
        for p in range(GROUPS):
            k = lax.rem(q + offs[p], n)
            dist = jnp.minimum(lax.rem(k - z + n, n), lax.rem(z - k + n, n))

            @pl.when(dist == far)
            def _():
                place = xg.at[k * 2 * GROUPS + e * GROUPS + p]
                pltpu.make_async_copy(x_ref.at[p], place, x_rs.at[k]).start()

                for i in FAR_FIRST:
                    remote(x_ref.at[p], place, x_ss, x_rs.at[k], peer(i)).start()

    def forward(k):
        held = xg.at[pl.ds(k * 2 * GROUPS + e * GROUPS, GROUPS)]
        drain(held, x_rs.at[k])
        remote(held, held, f_ss, f_rs.at[k], sibling).start()

    def columns(tile):
        return jnp.concatenate([tile[:, g : g + 1][None] for g in range(2 * GROUPS)], axis=0)

    def centered(k, d):
        at = pl.ds(k * 2 * GROUPS, 2 * GROUPS)
        x = xg[at].astype(F32)
        mean = jnp.sum(x, axis=2, keepdims=True) * (1.0 / feat)
        x = x - mean
        square = jnp.sum(x * x, axis=2, keepdims=True)
        m_tile = jnp.zeros((8, 128), F32)
        s_tile = jnp.zeros((8, 128), F32)
        for g in range(2 * GROUPS):
            m_tile = jnp.where(lane == g, mean[g], m_tile)
            s_tile = jnp.where(lane == g, square[g], s_tile)
        lm[d] = m_tile
        lm2[d] = s_tile
        return (x * gain_ref[...][None]).reshape(rows, feat).astype(BF16)

    def chunk(d, s):
        return lax.rem(z + n + half - s, n) if d == 0 else lax.rem(z + half + s, n)

    def wait_inputs(k):
        drain(xg.at[pl.ds(k * 2 * GROUPS, GROUPS)], f_rs.at[k])

    def products(s):
        wait_inputs(chunk(0, s))

        @pl.when(s < half)
        def _():
            wait_inputs(chunk(1, s))

        both = jnp.concatenate([centered(chunk(0, s), 0), centered(chunk(1, s), 1)], axis=0)
        for i in range(3):
            cols = slice(i * (unit // 3), (i + 1) * (unit // 3))
            pbuf[:, cols] = jnp.dot(both, wu[:, cols], preferred_element_type=F32)

    def st_copy(d, s):
        return remote(st_out.at[d, s], st_in.at[d, s], st_ss, st_rs.at[d, s], along[d])

    def rs_copy(d, s, j):
        at = (d * half + s) * J + j
        return remote(rs_out.at[at], rs_in.at[at], r_ss, r_rs.at[d, s, j], along[d])

    def gb_copy(d, s, src):
        return remote(src, gb_in.at[d * half + s], gb_ss, gb_rs.at[d, s], along[d])

    def row_of(ref_value, first, j):
        per = width // 128
        return jnp.concatenate(
            [ref_value[first + j * per + i : first + j * per + i + 1] for i in range(per)], axis=1
        )

    per_row = unit // 128
    gb_rows[...] = jnp.zeros_like(gb_rows)
    zero = jnp.zeros((rows, width), BF16)
    for d in range(2):
        for j in SPLIT[1 - d]:
            rs_in[d * half * J + j] = zero

    load_x.wait()
    def spread_all(i, carry):
        spread(half - i)
        return carry

    lax.fori_loop(0, half + 1, spread_all, 0)

    for load in load_rows:
        load.wait()
    load_up.wait()
    first = chunk(0, 0)
    forward(first)
    wait_inputs(first)
    start = centered(first, 0)
    st_out[0, 0] = lm[0] + pltpu.roll(lm2[0], 64, 1)
    st_out[1, 0] = lm[0]
    for d in range(2):
        st_copy(d, 0).start()
    for i in range(2):
        for d in range(2):
            j = SPLIT[d][i]
            part = jnp.dot(start, wu[:, j * width : (j + 1) * width], preferred_element_type=F32)
            rs_out[d * half * J + j] = part.astype(BF16)
            rs_copy(d, 0, j).start()
    for s in (1, 2):
        for d in range(2):
            forward(chunk(d, s))
    sub = lax.broadcasted_iota(jnp.int32, (16, feat), 0)
    gain, bias = gain_ref[...], bias_ref[...]
    gain_hi, bias_hi = gain.astype(BF16).astype(F32), bias.astype(BF16).astype(F32)
    lhs = jnp.where(
        sub == 0,
        gain_hi,
        jnp.where(
            sub == 1,
            gain - gain_hi,
            jnp.where(sub == 2, bias_hi, jnp.where(sub == 3, bias - bias_hi, 0.0)),
        ),
    ).astype(BF16)
    sums = jnp.dot(lhs, wu[...], preferred_element_type=F32)
    for i in range(per_row):
        cols = slice(i * 128, (i + 1) * 128)
        gb_rows[i : i + 1] = sums[0:1, cols] + sums[1:2, cols]
        gb_rows[per_row + i : per_row + i + 1] = sums[2:3, cols] + sums[3:4, cols]
    gb[...] = gb_rows[...].astype(BF16)
    for d in range(2):
        gb_copy(d, 0, gb).start()
    own_row = jnp.concatenate([gb_rows[i : i + 1] for i in range(per_row)], axis=1)

    def shifted(s):
        for d in range(2):
            st_copy(d, s - 1).wait_recv()
            got = st_in[d, s - 1]
            off = jnp.where(head, lm[d] - got, 0.0)

            @pl.when(s < half)
            def _():
                square = jnp.where(head, lm2[d] + feat * off * off, 0.0)
                st_out[d, s] = got + pltpu.roll(off, 32, 1) + pltpu.roll(square, 64, 1)
                st_copy(d, s).start()

            off_c = columns(off)
            for j in range(J):
                cols = slice(j * width, (j + 1) * width)
                at = slice(d * rows, (d + 1) * rows)
                mine = pbuf[at, cols].reshape(2 * GROUPS, 8, width) + off_c * own_row[:, cols][None]
                pbuf[at, cols] = mine.reshape(rows, width)

    products(1)
    shifted(1)

    def rs_step(s, carry):
        for i in range(J):
            for d in range(2):
                j = RS_ORDER[d][i]
                if j in SPLIT[1 - d]:
                    pl.when(s > 1)(lambda d=d, j=j: rs_copy(d, s - 1, j).wait_recv())
                else:
                    rs_copy(d, s - 1, j).wait_recv()
                got = rs_in[(d * half + s - 1) * J + j].astype(F32).reshape(2 * GROUPS, 8, width)
                mine = pbuf[d * rows : (d + 1) * rows, j * width : (j + 1) * width]
                total = got + mine.reshape(2 * GROUPS, 8, width)
                rs_out[(d * half + s) * J + j] = total.reshape(rows, width).astype(BF16)
                rs_copy(d, s, j).start()
        gb_copy(0, s - 1, gb).wait_recv()
        gb_copy(0, s, gb_in.at[s - 1]).start()
        gb_copy(1, s - 1, gb).wait_recv()

        @pl.when(s < half - 1)
        def _():
            gb_copy(1, s, gb_in.at[half + s - 1]).start()

        pl.when(s < half - 1)(lambda: forward(chunk(0, s + 2)))
        pl.when(s < half - 2)(lambda: forward(chunk(1, s + 2)))
        products(s + 1)
        shifted(s + 1)
        return carry

    lax.fori_loop(1, half, rs_step, 0)

    def ag_copy(d, s, j, src):
        at = (d * half + s) * J + j
        return remote(src, ag_in.at[at], a_ss, a_rs.at[d, s, j], along[d])

    gb_copy(0, half - 1, gb).wait_recv()
    load_down.wait()
    gb_all = gb_rows[...]
    for i in range(2 * half - 1):
        gb_all = gb_all + gb_in[i].astype(F32)
    up, down = st_in[0, half - 1], st_in[1, half - 1]
    off = jnp.where(head, lm[0] - up, 0.0)
    mean_off = (pltpu.roll(up + down, 96, 1) + off) * (1.0 / n)
    square = pltpu.roll(up + down, 64, 1) + lm2[0] + feat * off * off
    scale = lax.rsqrt(square * (1.0 / (n * feat)) - mean_off * mean_off + EPS)
    mean_c, scale_c = columns(mean_off), columns(scale)
    for j in LAST_ORDER:
        cols = slice(j * width, (j + 1) * width)
        total = pbuf[0:rows, cols].reshape(2 * GROUPS, 8, width)
        for d in range(2):
            rs_copy(d, half - 1, j).wait_recv()
            got = rs_in[(d * half + half - 1) * J + j]
            total = total + got.astype(F32).reshape(2 * GROUPS, 8, width)
        total = total - mean_c * row_of(gb_all, 0, j)[None]
        v = total * scale_c + row_of(gb_all, per_row, j)[None] + ub_ref[:, cols][None]
        hidden = jax.nn.gelu(v, approximate=True)
        ag_own[j] = hidden.reshape(rows, width).astype(BF16)
        for d in range(2):
            ag_copy(d, 0, j, ag_own.at[j]).start()

    def pair_copy(k):
        return remote(pair_out.at[k], pair_in.at[k], p_ss, p_rs.at[k], sibling)

    def to_pair(k, value):
        tb[k] = value.reshape(2 * GROUPS, 8, feat)
        pair_out[k] = tb[k, pl.ds((1 - e) * GROUPS, GROUPS)].astype(BF16)
        pair_copy(k).start()

    def to_owner(k):
        pair_copy(k).wait_recv()
        star_out[k] = (tb[k, pl.ds(e * GROUPS, GROUPS)] + pair_in[k].astype(F32)).astype(BF16)
        for p in range(GROUPS):
            owner = lax.rem(k - offs[p] + n, n)
            place = star_in.at[p * n + q]

            @pl.when(owner == q)
            def _():
                pltpu.make_async_copy(star_out.at[k, p], place, s_rs).start()

            @pl.when(owner != q)
            def _():
                remote(star_out.at[k, p], place, s_ss, s_rs, (z, 2 * owner + e)).start()

    def down_product(pieces):
        return jnp.dot(jnp.concatenate(pieces, axis=1), wd[...], preferred_element_type=F32)

    to_pair(z, down_product([ag_own[j] for j in range(J)]))

    def ag_step(s, carry):
        for i in range(J):
            for d in range(2):
                j = AG_ORDER[d][i]
                ag_copy(d, s, j, ag_own.at[j]).wait_recv()
                held = ag_in.at[(d * half + s) * J + j]
                if j in SPLIT[d]:
                    ag_copy(d, s + 1, j, held).start()
                else:
                    pl.when(s < half - 2)(lambda d=d, j=j, held=held: ag_copy(d, s + 1, j, held).start())
        to_owner(lax.rem(z - s + n, n))
        pl.when(s > 0)(lambda: to_owner(lax.rem(z + s, n)))
        value = down_product(
            [
                jnp.concatenate([ag_in[s * J + j], ag_in[(half + s) * J + j]], axis=0)
                for j in range(J)
            ]
        )
        to_pair(lax.rem(z - 1 - s + n, n), value[:rows])
        to_pair(lax.rem(z + 1 + s, n), value[rows:])
        return carry

    lax.fori_loop(0, half - 1, ag_step, 0)
    to_owner(lax.rem(z + 1 + half, n))
    to_owner(lax.rem(z + half - 1, n))
    last = lax.rem(z + half, n)
    value = jnp.zeros((rows, feat), F32)
    for i in range(2):
        for d in range(2):
            j = SPLIT[d][i]
            ag_copy(d, half - 1, j, ag_own.at[j]).wait_recv()
            value = value + jnp.dot(
                ag_in[(d * half + half - 1) * J + j],
                wd[j * width : (j + 1) * width],
                preferred_element_type=F32,
            )
    to_pair(last, value)
    to_owner(last)

    drain(star_in, s_rs)
    for p in range(GROUPS):
        total = jnp.sum(star_in[p * n : (p + 1) * n].astype(F32), axis=0)
        out_ref[p] = (x_ref[p].astype(F32) + total + db_ref[...]).astype(BF16)

    drain(xg.at[pl.ds(0, GROUPS * (n - 1))], x_ss)
    drain(xg.at[pl.ds(0, GROUPS * n)], f_ss)
    drain(st_in, st_ss)
    drain(gb_in.at[pl.ds(0, n - 1)], gb_ss)
    drain(rs_in.at[pl.ds(0, (n - 1) * J)], r_ss)
    drain(ag_in.at[pl.ds(0, (n - 1) * J)], a_ss)
    drain(pair_in, p_ss)
    drain(star_in.at[pl.ds(0, GROUPS * (n - 1))], s_ss)


def local(n, inputs, ln_gain, ln_bias, w_up, up_bias, w_down, down_bias):
    feat, unit = w_up.shape
    half, rows, width = n // 2, 2 * GROUPS * 8, unit // J
    tall = (2 * unit // 128 + 15) // 16 * 16
    vmem, hbm = pl.BlockSpec(memory_space=pltpu.VMEM), pl.BlockSpec(memory_space=pltpu.HBM)
    sem = pltpu.SemaphoreType.DMA
    out = pl.pallas_call(
        functools.partial(kernel, n),
        out_shape=jax.ShapeDtypeStruct((GROUPS, 8, feat), BF16),
        in_specs=[hbm] * 7,
        out_specs=vmem,
        scratch_shapes=[
            pltpu.VMEM((GROUPS, 8, feat), BF16),
            pltpu.VMEM((1, feat), F32),
            pltpu.VMEM((1, feat), F32),
            pltpu.VMEM((1, unit), F32),
            pltpu.VMEM((1, feat), F32),
            pltpu.VMEM((feat, unit), BF16),
            pltpu.VMEM((unit, feat), BF16),
            pltpu.VMEM((n * 2 * GROUPS, 8, feat), BF16),
            pltpu.VMEM((2 * rows, unit), F32),
            pltpu.VMEM((2, 8, 128), F32),
            pltpu.VMEM((2, 8, 128), F32),
            pltpu.VMEM((2, half, 8, 128), F32),
            pltpu.VMEM((2, half, 8, 128), F32),
            pltpu.VMEM((tall, 128), F32),
            pltpu.VMEM((tall, 128), BF16),
            pltpu.VMEM((n, tall, 128), BF16),
            pltpu.VMEM((2 * half * J, rows, width), BF16),
            pltpu.VMEM((2 * half * J, rows, width), BF16),
            pltpu.VMEM((J, rows, width), BF16),
            pltpu.VMEM((2 * half * J, rows, width), BF16),
            pltpu.VMEM((n, 2 * GROUPS, 8, feat), F32),
            pltpu.VMEM((n, GROUPS, 8, feat), BF16),
            pltpu.VMEM((n, GROUPS, 8, feat), BF16),
            pltpu.VMEM((n, GROUPS, 8, feat), BF16),
            pltpu.VMEM((GROUPS * n, 8, feat), BF16),
            sem((7,)),
            sem,
            sem((n,)),
            sem,
            sem((n,)),
            sem,
            sem((2, half)),
            sem,
            sem((2, half)),
            sem,
            sem((2, half, J)),
            sem,
            sem((2, half, J)),
            sem,
            sem((n,)),
            sem,
            sem,
        ],
        compiler_params=pltpu.CompilerParams(
            collective_id=0, has_side_effects=True, vmem_limit_bytes=50 << 20
        ),
    )(
        *(
            pltpu.with_memory_space_constraint(a, pltpu.HBM)
            for a in (
                inputs.reshape(GROUPS, 8, feat),
                ln_gain,
                ln_bias,
                up_bias,
                down_bias,
                w_up,
                w_down,
            )
        )
    )
    return out.reshape(GROUPS * 8, feat)


def solution(mesh):
    placed = (
        P("col", "row"),
        P("row"),
        P("row"),
        P("row", "col"),
        P("col"),
        P("col", "row"),
        P("row"),
    )
    return jax.shard_map(
        functools.partial(local, mesh.shape["row"]),
        mesh=mesh,
        in_specs=placed,
        out_specs=P("col", "row"),
        check_vma=False,
    )
```
